256 devices in a mesh: gx: 4 (over y), gy: 8 (over z_lo, x), gz: 8 (over z_hi, core).
Axes of the slice: x: 4, y: 4, z: 8 (z_hi: 4, z_lo: 2; z = z_hi * 2 + z_lo), core: 2. Of those that a mesh axis runs over, the one named last changes fastest.
Arguments:
- saved_input: bfloat16 [1536, 12288], P('gx', ('gy', 'gz')), may hold values from -6 to 6
- weight: bfloat16 [12288, 24576], P('gy', ('gz', 'gx')), may hold values from -0.0546875 to 0.0546875
- out_grad: bfloat16 [1536, 24576], P('gx', ('gz', 'gy')), may hold values from -16 to 16
Outputs:
- input_grad: bfloat16 [1536, 12288], P('gx', ('gy', 'gz'))
- weight_grad: bfloat16 [12288, 24576], P('gy', ('gz', 'gx'))
The draws below stay inside these ranges and needn't reach their ends.
All inputs are finite; a program needn't handle non-finite values.
Results may differ from the reference program's by a relative error of at most 0.022.
Values may be sent and summed in bfloat16 or wider, within the bound.
A program may use at most 128 MiB of HBM per device.

```python
import jax
import jax.numpy as jnp
from jax import lax

D = 12288
FF = 24576
TOK_DEV = 384
TOKENS = 1536
N_GX = 4


def raised(entries, key, source, target, blocks, factor):
    owner, partner = [(jnp.arange(entries.shape[axis_at]) // (entries.shape[axis_at] // blocks)).reshape([-1 if axis == axis_at else 1 for axis in range(entries.ndim)]) for axis_at in (source, target)]
    chosen = jax.random.permutation(key, blocks)[partner]
    strong = (owner == chosen) | (owner == (partner + blocks // 2) % blocks)
    return jnp.where(strong, factor * entries, entries)


def block_scale(rng, extent, pieces, smallest, high):
    loudness, own = 1.0, jax.random.fold_in(rng, 6)
    for axis_at, shards_of in pieces:
        draws = jnp.exp(jax.random.uniform(jax.random.fold_in(own, axis_at), (shards_of,), jnp.float32, smallest / len(pieces), high / len(pieces)))
        loudness = loudness * jnp.repeat(draws, extent[axis_at] // shards_of).reshape([-1 if axis == axis_at else 1 for axis in range(len(extent))])
    return loudness


def normal_values(own_key, dims, spread, most, cuts=(), kind=jnp.bfloat16):
    gain = block_scale(own_key, dims, cuts, -0.22, 0.18) if cuts else 1.0
    entries = jax.random.normal(own_key, dims, jnp.float32) * spread * gain
    return jnp.minimum(jnp.maximum(entries, -most), most).astype(kind)


def gaussian_with(own_key, extent, deviation, limit, pieces, heavy, held_as=jnp.bfloat16):
    array = deviation * jax.random.normal(own_key, extent, jnp.float32)
    if pieces:
        array = array * block_scale(own_key, extent, pieces, -0.22, 0.18)
    return jnp.clip(raised(array, jax.random.fold_in(own_key, 3), *heavy), -limit, limit).astype(held_as)


def setup_inputs(seed: int = 0) -> dict:
    splits = jax.random.split(jax.random.key(seed), 4)
    saved_input = normal_values(splits[0], (TOKENS, D), 1.0, 6.0, ((0, 4), (1, 64)))
    weight = normal_values(splits[1], (D, FF), D ** -0.5, 0.0546875, ((0, 8), (1, 32)))
    out_grad = gaussian_with(splits[2], (TOKENS, FF), 1.0, 16.0, ((0, 4), (1, 64)), (0, 1, 64, 4.0))
    return dict(saved_input=saved_input, weight=weight, out_grad=out_grad)


def gelu_slope(pre, grad):
    _, pullback = jax.vjp(lambda values: jax.nn.gelu(values, approximate=True), pre)
    return pullback(grad.astype(jnp.float32))[0]

def reference(saved_input, weight, out_grad):
    pre = jnp.dot(saved_input, weight, preferred_element_type=jnp.float32)
    pre_grad = gelu_slope(pre, out_grad).astype(jnp.bfloat16)
    input_grad = lax.dot_general(pre_grad, weight, (((1,), (1,)), ((), ())), preferred_element_type=jnp.float32).astype(jnp.bfloat16)

    def add_block(index, totals):
        start = (index * TOK_DEV).astype(jnp.int32)
        rows_in = lax.dynamic_slice_in_dim(saved_input, start, TOK_DEV, 0)
        rows_grad = lax.dynamic_slice_in_dim(pre_grad, start, TOK_DEV, 0)
        term = lax.dot_general(rows_in, rows_grad, (((0,), (0,)), ((), ())), preferred_element_type=jnp.float32)
        return totals + term.astype(jnp.bfloat16).astype(jnp.float32)
    totals = lax.fori_loop(jnp.int32(0), jnp.int32(N_GX), add_block, jnp.zeros((D, FF), jnp.float32))
    return (input_grad, totals.astype(jnp.bfloat16))
```

```python
import jax
import jax.numpy as jnp
from jax import lax
from jax.sharding import PartitionSpec as P


def gelu_slope(pre, grad):
    _, pullback = jax.vjp(lambda values: jax.nn.gelu(values, approximate=True), pre)
    return pullback(grad.astype(jnp.float32))[0]


def local(saved_input, weight, out_grad):
    feats = lax.all_gather(saved_input, "gz", axis=1, tiled=True)
    inputs = lax.all_gather(feats, "gx", axis=0, tiled=True)
    partial_value = jnp.dot(inputs, weight, preferred_element_type=jnp.float32).astype(jnp.bfloat16)
    pieces = partial_value.reshape(4, 384, 2, 384).transpose(0, 2, 1, 3).reshape(8 * 384, 384)
    pre = lax.psum_scatter(pieces, "gy", scatter_dimension=0, tiled=True).astype(jnp.float32)
    perm = [(t * 8 + 2 * a + h, a * 8 + 2 * t + h) for t in range(4) for a in range(4) for h in range(2)]
    grad = lax.ppermute(out_grad, ("gx", "gy"), perm)
    piece_grad = gelu_slope(pre, grad).astype(jnp.bfloat16)
    gathered = lax.all_gather(piece_grad, "gy", axis=0, tiled=True)
    pre_grad = gathered.reshape(4, 2, 384, 384).transpose(0, 2, 1, 3).reshape(1536, 768)
    input_terms = lax.dot_general(
        pre_grad, weight, (((1,), (1,)), ((), ())), preferred_element_type=jnp.float32
    ).astype(jnp.bfloat16)
    by_token = lax.psum_scatter(input_terms, "gx", scatter_dimension=0, tiled=True)
    input_grad = lax.psum_scatter(by_token, "gz", scatter_dimension=1, tiled=True)
    weight_grad = lax.dot_general(
        inputs, pre_grad, (((0,), (0,)), ((), ())), preferred_element_type=jnp.float32
    ).astype(jnp.bfloat16)
    return (input_grad, weight_grad)


def solution(mesh):
    placed = (P("gx", ("gy", "gz")), P("gy", ("gz", "gx")), P("gx", ("gz", "gy")))
    return jax.shard_map(
        local,
        mesh=mesh,
        in_specs=placed,
        out_specs=(P("gx", ("gy", "gz")), P("gy", ("gz", "gx"))),
        check_vma=False,
    )
```

```python
import jax
import jax.numpy as jnp
from jax import lax
from jax.experimental import pallas as pl
from jax.experimental.pallas import tpu as pltpu
from jax.sharding import PartitionSpec as P

MESH = pl.DeviceIdType.MESH
F32 = jnp.float32
BF16 = jnp.bfloat16
ROOT = 0.7978845608028654
CUBE = 0.044715
N_SEM = 160


def gelu_slope(pre, grad):
    square = pre * pre
    tanh = jnp.tanh(ROOT * (pre + CUBE * (pre * square)))
    slope = 0.5 * (1.0 + tanh) + (0.5 * ROOT) * pre * (1.0 - tanh * tanh) * (1.0 + 3.0 * CUBE * square)
    return grad * slope


def kernel(x_ref, w_hbm, g_ref, dx_out, dw_out,
           wv, wt, gt, gl, xt, pp, rz, s1, rx, pt, dx, rc, sy, ry, sz, rzz, dwv,
           ssem, rsem, lsem):
    y, gy, gz = lax.axis_index("gx"), lax.axis_index("gy"), lax.axis_index("gz")
    zl, x = gy // 4, gy % 4
    zh, c = gz // 2, gz % 2

    core = (y, gy, zh * 2 + (1 - c))
    zlp = (y, (1 - zl) * 4 + x, gz)

    def on_y(d):
        return ((y + d) % 4, gy, gz)

    def on_x(d):
        return (y, zl * 4 + (x + d) % 4, gz)

    def on_z(d):
        return (y, gy, ((zh + d) % 4) * 2 + c)

    g_dst = [(2 * zl + x // 2, z * 4 + 2 * (x % 2) + k, gz) for k in range(2) for z in range(2)]
    g_rows = [(2 * k + z) * 96 for k in range(2) for z in range(2)]
    g_src = [(t, (y // 2) * 4 + 2 * (y % 2) + x // 2, gz) for t in range(4)]
    own_g = jnp.logical_and(zl == y // 2, x == 2 * (y % 2) + x // 2)
    count = [0]
    sends = []

    def slot():
        count[0] += 1
        return count[0] - 1

    def send(src, dst, to, k):
        cp = pltpu.make_async_remote_copy(src, dst, ssem.at[k], rsem.at[k], device_id=to, device_id_type=MESH)
        cp.start()
        sends.append(cp)

    def arrived(dst, k):
        pltpu.make_async_remote_copy(dst, dst, ssem.at[k], rsem.at[k], device_id=core, device_id_type=MESH).wait_recv()

    w_copy = pltpu.make_async_copy(w_hbm, wv, lsem.at[0])
    w_copy.start()
    x_copy = pltpu.make_async_copy(x_ref, xt.at[0, zh, c], lsem.at[1])
    x_copy.start()

    barrier = pltpu.get_barrier_semaphore()
    partners = [core, zlp] + [on_y(d) for d in (1, 2, 3)] + [on_x(d) for d in (1, 2, 3)] + [on_z(d) for d in (1, 2, 3)]
    for p in partners:
        pl.semaphore_signal(barrier, inc=1, device_id=p, device_id_type=MESH)
    for t in range(4):
        @pl.when(jnp.logical_not(jnp.logical_and(own_g, y == t)))
        def _(t=t):
            pl.semaphore_signal(barrier, inc=1, device_id=g_src[t], device_id_type=MESH)
    pl.semaphore_wait(barrier, len(partners) + 4 - own_g.astype(jnp.int32))

    k_z = [None] + [slot() for _ in range(3)]
    k_c0 = [slot() for _ in range(4)]
    k_y = [[slot() for _ in range(4)] for _ in range(2)]
    k_cy = [[slot() for _ in range(4)] for _ in range(2)]
    k_f = [[slot() for _ in range(4)] for _ in range(2)]
    k_cf = [[slot() for _ in range(4)] for _ in range(2)]

    def zof(d):
        return (zh - d + 4) % 4

    for d in (2, 1, 3):
        send(x_ref, xt.at[0, zh, c], on_z(d), k_z[d])
    send(x_ref, xt.at[3, zh, c], on_y(1), k_y[0][0])
    send(x_ref, xt.at[1, zh, c], on_y(3), k_y[1][0])
    send(x_ref, xt.at[0, zh, c], core, k_c0[0])

    gt[...] = g_ref[...].T
    k_g = [slot() for _ in range(4)]
    g_sends = []
    for n in range(4):
        a, dgy, _ = g_dst[n]
        r = (y - a + 4) % 4
        here = jnp.logical_and(a == y, dgy == gy)
        src = gt.at[pl.ds(g_rows[n], 96)]
        cp = pltpu.make_async_remote_copy(src, gl.at[r], ssem.at[k_g[n]], rsem.at[k_g[0] + r], device_id=g_dst[n], device_id_type=MESH)
        lp = pltpu.make_async_copy(src, gl.at[0], lsem.at[2])

        @pl.when(jnp.logical_not(here))
        def _(cp=cp):
            cp.start()

        @pl.when(here)
        def _(lp=lp):
            lp.start()
        g_sends.append((here, cp, lp))

    w_copy.wait()

    @pl.loop(0, 6)
    def _(i):
        rows = pl.ds(pl.multiple_of(i * 256, 256), 256)
        wt[:, rows] = wv[rows, :].T

    x_copy.wait()

    def pass_y(d):
        z = zof(d)
        arrived(xt.at[3, z, c], k_y[0][d])
        send(xt.at[3, z, c, pl.ds(0, 96)], xt.at[2, z, c, pl.ds(0, 96)], on_y(1), k_f[0][d])
        send(xt.at[3, z, c], xt.at[3, z, c], core, k_cy[0][d])
        arrived(xt.at[1, z, c], k_y[1][d])
        send(xt.at[1, z, c, pl.ds(96, 96)], xt.at[2, z, c, pl.ds(96, 96)], on_y(3), k_f[1][d])
        send(xt.at[1, z, c], xt.at[1, z, c], core, k_cy[1][d])

    pass_y(0)
    for d in (1, 3, 2):
        z = zof(d)
        arrived(xt.at[0, z, c], k_z[d])
        send(xt.at[0, z, c], xt.at[3, z, c], on_y(1), k_y[0][d])
        send(xt.at[0, z, c], xt.at[1, z, c], on_y(3), k_y[1][d])
        send(xt.at[0, z, c], xt.at[0, z, c], core, k_c0[d])

    def term(r):
        block = xt[r].reshape(1536, 384)

        @pl.loop(0, 4)
        def _(i):
            rows = pl.ds(pl.multiple_of(i * 192, 192), 192)
            pp[r, i] = jnp.dot(wt[rows, :], block, preferred_element_type=F32).astype(BF16).reshape(2, 96, 384)

    k_rz = [slot() for _ in range(4)]
    k_rx = [[None] + [slot() for _ in range(3)] for _ in range(4)]
    k_pz = [slot() for _ in range(4)]
    k_px = [[None] + [slot() for _ in range(3)] for _ in range(4)]
    k_rc = [slot() for _ in range(4)]
    k_ry = [None] + [[slot() for _ in range(4)] for _ in range(3)]
    k_rzz = [None] + [slot() for _ in range(3)]

    def step_a(r):
        term(r)
        send(pp.at[r, :, 1 - zl], rz.at[r], zlp, k_rz[r])

    def step_b(r):
        arrived(rz.at[r], k_rz[r])
        s1[r] = (pp[r, :, zl].astype(F32) + rz[r].astype(F32)).astype(BF16)
        for d in (2, 1, 3):
            send(s1.at[r, (x + d) % 4], rx.at[r, d - 1], on_x(d), k_rx[r][d])

    def step_c(r):
        total = s1[r, x].astype(F32)
        for d in (1, 3, 2):
            arrived(rx.at[r, d - 1], k_rx[r][d])
            total = total + rx[r, d - 1].astype(F32)
        pt[r, x, zl] = gelu_slope(total, gl[r].astype(F32)).astype(BF16)
        send(pt.at[r, x, zl], pt.at[r, x, zl], zlp, k_pz[r])

    def step_d(r):
        arrived(pt.at[r, x, 1 - zl], k_pz[r])
        for d in (2, 1, 3):
            send(pt.at[r, x], pt.at[r, x], on_x(d), k_px[r][d])

    def step_e(r):
        for d in (1, 3, 2):
            arrived(pt.at[r, (x - d + 4) % 4], k_px[r][d])
        block = pt[r].reshape(768, 384)

        @pl.loop(0, 4)
        def _(i):
            rows = pl.ds(pl.multiple_of(i * 384, 384), 384)
            dx[r, i] = jnp.dot(wv[rows, :], block, preferred_element_type=F32).astype(BF16).reshape(2, 192, 384)
        send(dx.at[r, :, 1 - c], rc.at[r], core, k_rc[r])

    def step_f(r):
        arrived(rc.at[r], k_rc[r])
        sy[r] = (dx[r, :, c].astype(F32) + rc[r].astype(F32)).astype(BF16)
        if r:
            for d in (2, 1, 3, 0):
                z = (zh + d) % 4
                send(sy.at[r, z], ry.at[r - 1, z], on_y(r), k_ry[r][d])

    def core_wait(r):
        if r == 0:
            for d in (0, 1, 3, 2):
                arrived(xt.at[0, zof(d), 1 - c], k_c0[d])
        elif r == 2:
            for d in (0, 1, 3, 2):
                arrived(xt.at[2, zof(d), 1 - c, pl.ds(0, 96)], k_cf[0][d])
                arrived(xt.at[2, zof(d), 1 - c, pl.ds(96, 96)], k_cf[1][d])
        else:
            for d in (0, 1, 3, 2):
                arrived(xt.at[r, zof(d), 1 - c], k_cy[0 if r == 3 else 1][d])

    core_wait(0)
    step_a(0)
    for d in (1, 3, 2):
        pass_y(d)
    step_b(0)
    core_wait(3)
    step_a(3)
    core_wait(1)
    step_a(1)
    for n in range(4):
        here, cp, lp = g_sends[n]

        @pl.when(here)
        def _(lp=lp):
            lp.wait()

    for r in range(4):
        if r == 0:
            @pl.when(jnp.logical_not(own_g))
            def _():
                arrived(gl.at[0], k_g[0])
        else:
            arrived(gl.at[r], k_g[r])
    step_c(0)
    for d in (0, 1, 3, 2):
        z = zof(d)
        for half in range(2):
            part = xt.at[2, z, c, pl.ds(half * 96, 96)]
            arrived(part, k_f[half][d])
            send(part, part, core, k_cf[half][d])
    step_b(3)
    step_b(1)
    core_wait(2)
    step_a(2)
    step_c(3)
    step_d(0)
    step_c(1)
    step_b(2)
    step_d(3)
    step_d(1)
    step_c(2)
    step_d(2)
    step_e(3)
    step_e(1)
    step_f(3)
    step_f(1)
    step_e(2)
    step_e(0)
    step_f(2)
    step_f(0)

    @pl.loop(0, 4)
    def _(i):
        total = None
        for r in range(4):
            one = lax.dot_general(xt[r, i].reshape(384, 384), pt[r].reshape(768, 384), (((1,), (1,)), ((), ())),
                                  preferred_element_type=F32)
            total = one if total is None else total + one
        dwv[pl.ds(pl.multiple_of(i * 384, 384), 384), :] = total.astype(BF16)
    dw_copy = pltpu.make_async_copy(dwv, dw_out, lsem.at[3])
    dw_copy.start()

    total = None
    for d in (2, 1, 3, 0):
        z = (zh + d) % 4
        part = sy[0, z].astype(F32)
        for r in (3, 1, 2):
            arrived(ry.at[r - 1, z], k_ry[r][d])
            part = part + ry[r - 1, z].astype(F32)
        if d:
            sz[d - 1] = part.astype(BF16)
            send(sz.at[d - 1], rzz.at[d - 1], on_z(d), k_rzz[d])
        else:
            total = part
    for d in (1, 3, 2):
        arrived(rzz.at[d - 1], k_rzz[d])
        total = total + rzz[d - 1].astype(F32)
    dx_out[...] = total.astype(BF16)

    for cp in sends:
        cp.wait_send()
    for here, cp, lp in g_sends:
        @pl.when(jnp.logical_not(here))
        def _(cp=cp):
            cp.wait_send()
    dw_copy.wait()
    assert count[0] <= N_SEM, count


def local(saved_input, weight, out_grad):
    vmem = pl.BlockSpec(memory_space=pltpu.VMEM)
    scratch = [
        (1536, 768), (768, 1536), (384, 384), (4, 96, 384),
        (4, 4, 2, 192, 384),
        (4, 4, 2, 96, 384), (4, 4, 96, 384), (4, 4, 96, 384),
        (4, 3, 96, 384), (4, 4, 2, 96, 384),
        (4, 4, 2, 192, 384), (4, 4, 192, 384), (4, 4, 192, 384),
        (3, 4, 192, 384), (3, 192, 384), (3, 192, 384),
        (1536, 768),
    ]
    dx, dw = pl.pallas_call(
        kernel,
        out_shape=[jax.ShapeDtypeStruct((192, 384), BF16), jax.ShapeDtypeStruct((1536, 768), BF16)],
        in_specs=[vmem, pl.BlockSpec(memory_space=pl.ANY), vmem],
        out_specs=[vmem, pl.BlockSpec(memory_space=pl.ANY)],
        scratch_shapes=[pltpu.VMEM(s, BF16) for s in scratch] + [
            pltpu.SemaphoreType.DMA((N_SEM,)), pltpu.SemaphoreType.DMA((N_SEM,)), pltpu.SemaphoreType.DMA((4,))],
        compiler_params=pltpu.CompilerParams(collective_id=0, has_side_effects=True, vmem_limit_bytes=56 * 2**20),
        cost_estimate=pl.CostEstimate(flops=3 * 2 * 1536 * 1536 * 768, bytes_accessed=8 * 2**20, transcendentals=0),
        name="fused_layer",
    )(saved_input.T, weight, out_grad)
    return dx.T, dw


def solution(mesh):
    placed = (P("gx", ("gy", "gz")), P("gy", ("gz", "gx")), P("gx", ("gz", "gy")))
    return jax.shard_map(
        local,
        mesh=mesh,
        in_specs=placed,
        out_specs=(P("gx", ("gy", "gz")), P("gy", ("gz", "gx"))),
        check_vma=False,
    )
```

```python
import functools

import jax
import jax.numpy as jnp
from jax import lax
from jax.experimental import pallas as pl
from jax.experimental.pallas import tpu as pltpu
from jax.sharding import PartitionSpec as P

MESH = pl.DeviceIdType.MESH
F32 = jnp.float32
BF16 = jnp.bfloat16
ROOT = 0.7978845608028654
CUBE = 0.044715
N_RECV = 89
N_SEND = 56

PARTS = ((0, 128), (128, 256))
ORDER = (
    "P", "W", "Y00", "Z30", "Y01", "Z10", "Y30", "Z11", "Z20", "Z31", "Y10", "K00", "A00", "Y20", "Y11", "Z21",
    "G", "H01", "K10", "A10", "H00", "H20", "K01", "H30", "A01", "H10", "K30", "H11", "Y31", "A30", "B00", "Y21",
    "K20", "A20", "B10", "K31", "A31", "B20", "K11", "B30", "A11", "H31", "H21", "C10", "K21", "A21", "C20",
    "D10", "C30", "B11", "C00", "D20", "V10", "B01", "B21", "V20", "E10", "D30", "C11", "B31", "E20", "V30",
    "C21", "D21", "F20", "D00", "C01", "E30", "D11", "C31", "V00", "F10", "F30", "V21", "E21", "D31", "E00",
    "F21", "V31", "V11", "F00", "S20", "S30", "D01", "E11", "E31", "F11", "F31", "S10", "V01", "E01", "F01",
    "S21", "M0", "S11", "S00", "S31", "T0", "S01", "M1", "T1",
)
SUM = "dxzxdzzz"
GATHER = "tssstdtd"


def gelu_slope(pre, grad):
    square = pre * pre
    tanh = jnp.tanh(ROOT * (pre + CUBE * (pre * square)))
    slope = 0.5 * (1.0 + tanh) + (0.5 * ROOT) * pre * (1.0 - tanh * tanh) * (1.0 + 3.0 * CUBE * square)
    return grad * slope


def part_scratch(n):
    return dict(
        xt=(4, 4, 2, 192, n),
        pp=(4, 4, 2, 96, n),
        rz=(4, 4, 96, n), s1=(4, 4, 96, n), rx=(4, 3, 96, n),
        rx2=(4, 3, 2, 96, n), s2=(4, 2, 96, n), rz2=(4, 96, n), rw=(4, 2, 96, n), sw=(4, 2, 2, 96, n),
        rd=(4, 7, 96, n),
        pt=(4, 4, 2, 96, n),
        dx=(4, 4, 2, 192, n),
        rc=(4, 4, 192, n), sy=(4, 4, 192, n), ry=(2, 4, 192, n), rf=(2, 4, 96, n),
        sz=(4, 192, n), rzz=(4, 192, n),
    )


def kernel(order, sums, gathers, parts, x_hbm, w_hbm, g_hbm, dx_out, dw_out, gv, wv, wt, gt, gl, dwv, *refs):
    ssem, rsem, lsem, near = refs[-4:]
    names = list(part_scratch(0))
    at = [dict(zip(names, refs[p * len(names):])) for p in range(len(parts))]
    xt, pp, rz, s1, rx, rx2, s2, rz2, rw, sw, rd, pt, dx, rc, sy, ry, rf, sz, rzz = ([a[n] for a in at] for n in names)

    y, gy, gz = lax.axis_index("gx"), lax.axis_index("gy"), lax.axis_index("gz")
    zl, x = gy // 4, gy % 4
    zh, c = gz // 2, gz % 2

    core = (y, gy, zh * 2 + (1 - c))
    zlp = (y, (1 - zl) * 4 + x, gz)

    def on_y(d):
        return ((y + d) % 4, gy, gz)

    def on_x(d, e=0):
        return (y, ((zl + e) % 2) * 4 + (x + d) % 4, gz)

    def on_z(d):
        return (y, gy, ((zh + d) % 4) * 2 + c)

    def zof(d):
        return (zh - d + 4) % 4

    def xof(d):
        return (x - d + 4) % 4

    g_dst = [(2 * zl + x // 2, z * 4 + 2 * (x % 2) + k, gz) for k in range(2) for z in range(2)]
    g_rows = [(2 * k + z) * 96 for k in range(2) for z in range(2)]
    own_g = jnp.logical_and(zl == y // 2, x == 2 * (y % 2) + x // 2)

    keys, sends, pending, state = {}, [], {}, {}
    others = ((2, 1), (2, 0), (1, 1), (1, 0), (3, 1), (3, 0), (0, 1))

    def mode(table, r, p):
        return table[r * len(parts) + p]

    def slot(*key):
        return keys.setdefault(key, len(keys))

    def send_slot():
        if len(sends) >= N_SEND:
            sends[-N_SEND]()
        return ssem.at[len(sends) % N_SEND]

    def send(src, dst, to, *key):
        cp = pltpu.make_async_remote_copy(src, dst, send_slot(), rsem.at[slot(*key)], device_id=to, device_id_type=MESH)
        cp.start()
        sends.append(cp.wait_send)
        pending.setdefault(key, []).append(dst)

    def arrived(ref, *key):
        assert ref.size == sum(dst.size for dst in pending.pop(key))
        k = slot(*key)
        pltpu.make_async_remote_copy(ref, ref, ssem.at[0], rsem.at[k], device_id=core, device_id_type=MESH).wait_recv()

    barrier = pltpu.get_barrier_semaphore()
    partners = [core, zlp] + [on_y(d) for d in (1, 2, 3)] + [on_x(d) for d in (1, 2, 3)] + [on_z(d) for d in (1, 3)]
    for to in partners:
        pl.semaphore_signal(barrier, inc=1, device_id=to, device_id_type=MESH)
    x_copies = [pltpu.make_async_copy(x_hbm.at[:, pl.ds(t, n)], xt[p].at[0, zh, c], lsem.at[5 + p])
                for p, (t, n) in enumerate(parts)]
    g_copy = pltpu.make_async_copy(g_hbm, gv, lsem.at[4])
    w_copy = pltpu.make_async_copy(w_hbm, wv, lsem.at[0])
    for cp in x_copies + [g_copy, w_copy]:
        cp.start()

    pl.semaphore_wait(barrier, len(partners))
    for d in (1, 2, 3):
        pl.semaphore_signal(near.at[0], inc=1, device_id=on_x(d), device_id_type=MESH)

    halves = {1: pl.ds(0, 96), 3: pl.ds(96, 96)}

    def step_p():
        for p in range(len(parts)):
            x_copies[p].wait()
            own = xt[p].at[0, zh, c]
            send(own, own, on_z(1), "z", 1, p)
            send(own, own, on_z(3), "z", 3, p)
            send(own, xt[p].at[3, zh, c], on_y(1), "y", 3, 0, p)
            send(own, xt[p].at[1, zh, c], on_y(3), "y", 1, 0, p)
            send(own, own, core, "k", 0, p)

    def step_w():
        g_copy.wait()
        gt[...] = gv[...].T
        w_copy.wait()

        @pl.loop(0, 2)
        def _(i):
            rows = pl.ds(pl.multiple_of(i * 768, 768), 768)
            wt[:, rows] = wv[rows, :].T
        pl.semaphore_wait(near.at[0], 3)
        for d in (1, 2, 3):
            pl.semaphore_signal(near.at[1], inc=1, device_id=on_y(d), device_id_type=MESH)

    def step_g():
        pl.semaphore_wait(near.at[1], 3)
        state["g"] = []
        for n in range(4):
            a, dgy, _ = g_dst[n]
            r = (y - a + 4) % 4
            here = jnp.logical_and(a == y, dgy == gy)
            src = gt.at[pl.ds(g_rows[n], 96)]
            cp = pltpu.make_async_remote_copy(src, gl.at[r], send_slot(), rsem.at[slot("g")], device_id=g_dst[n], device_id_type=MESH)
            lp = pltpu.make_async_copy(src, gl.at[0], lsem.at[2])

            @pl.when(jnp.logical_not(here))
            def _(cp=cp):
                cp.start()

            @pl.when(here)
            def _(lp=lp):
                lp.start()

            def sent(here=here, cp=cp):
                @pl.when(jnp.logical_not(here))
                def _():
                    cp.wait_send()
            sends.append(sent)
            state["g"].append((here, lp))

    def g_wait():
        if "g" not in state:
            return
        for here, lp in state.pop("g"):
            @pl.when(here)
            def _(lp=lp):
                lp.wait()
        k = slot("g")

        @pl.when(own_g)
        def _():
            part = gl.at[pl.ds(1, 3)]
            pltpu.make_async_remote_copy(part, part, ssem.at[0], rsem.at[k], device_id=core, device_id_type=MESH).wait_recv()

        @pl.when(jnp.logical_not(own_g))
        def _():
            pltpu.make_async_remote_copy(gl, gl, ssem.at[0], rsem.at[k], device_id=core, device_id_type=MESH).wait_recv()

    def step_z(d, p):
        shard = (zof(d), c)
        here = xt[p].at[(0,) + shard]
        if d == 2:
            arrived(here, "zf", p)
        else:
            arrived(here, "z", d, p)
            half = xt[p].at[(0,) + shard + (halves[d],)]
            send(half, half, on_z(d), "zf", p)
        send(here, xt[p].at[(3,) + shard], on_y(1), "y", 3, d, p)
        send(here, xt[p].at[(1,) + shard], on_y(3), "y", 1, d, p)
        send(here, here, core, "k", 0, p)

    def step_y(d, p):
        shard = (zof(d), c)
        for r, to in ((3, 1), (1, 3)):
            here = xt[p].at[(r,) + shard]
            arrived(here, "y", r, d, p)
            send(xt[p].at[(r,) + shard + (halves[to],)], xt[p].at[(2,) + shard + (halves[to],)], on_y(to), "f", d, p)
            send(here, here, core, "k", r, p)

    def step_h(d, p):
        shard = (zof(d), c)
        here = xt[p].at[(2,) + shard]
        arrived(here, "f", d, p)
        send(here, here, core, "k", 2, p)

    def step_k(r, p):
        arrived(xt[p].at[r, :, 1 - c], "k", r, p)

    def step_a(r, p):
        n = parts[p][1]
        term = jnp.dot(wt[...], xt[p][r].reshape(1536, n), preferred_element_type=F32)
        pp[p][r] = term.astype(BF16).reshape(4, 2, 96, n)
        m = mode(sums, r, p)
        if m == "x":
            for d in (2, 1, 3):
                send(pp[p].at[r, (x + d) % 4], rx2[p].at[r, d - 1], on_x(d), "sx", r, p)
        elif m == "w":
            for k, d in enumerate((1, 3)):
                send(pp[p].at[r, (x + 2) % 4, k], rw[p].at[r, k], on_x(d), "sw", r, p)
        elif m == "z":
            send(pp[p].at[r, :, 1 - zl], rz[p].at[r], zlp, "sz", r, p)
        else:
            for i, (d, e) in enumerate(others):
                send(pp[p].at[r, (x + d) % 4, (zl + e) % 2], rd[p].at[r, i], on_x(d, e), "sd", r, p)

    def step_j(r, p):
        if mode(sums, r, p) == "w":
            arrived(rw[p].at[r], "sw", r, p)
            for k, d in enumerate((1, 3)):
                sw[p][r, k, k] = (pp[p][r, (x + d) % 4, k].astype(F32) + rw[p][r, k].astype(F32)).astype(BF16)
                sw[p][r, k, 1 - k] = pp[p][r, (x + d) % 4, 1 - k]
                send(sw[p].at[r, k], rx2[p].at[r, k], on_x(d), "sx", r, p)

    def step_b(r, p):
        m = mode(sums, r, p)
        if m in "xw":
            total = pp[p][r, x].astype(F32)
            came = 3 if m == "x" else 2
            arrived(rx2[p].at[r, pl.ds(0, came)], "sx", r, p)
            for i in range(came):
                total = total + rx2[p][r, i].astype(F32)
            s2[p][r] = total.astype(BF16)
            send(s2[p].at[r, 1 - zl], rz2[p].at[r], zlp, "sz", r, p)
        elif m == "z":
            arrived(rz[p].at[r], "sz", r, p)
            s1[p][r] = (pp[p][r, :, zl].astype(F32) + rz[p][r].astype(F32)).astype(BF16)
            for d in (2, 1, 3):
                send(s1[p].at[r, (x + d) % 4], rx[p].at[r, d - 1], on_x(d), "sx", r, p)

    def step_c(r, p):
        g_wait()
        m = mode(sums, r, p)
        if m in "xw":
            arrived(rz2[p].at[r], "sz", r, p)
            total = s2[p][r, zl].astype(F32) + rz2[p][r].astype(F32)
        elif m == "z":
            total = s1[p][r, x].astype(F32)
            arrived(rx[p].at[r], "sx", r, p)
            for i in range(3):
                total = total + rx[p][r, i].astype(F32)
        else:
            total = pp[p][r, x, zl].astype(F32)
            arrived(rd[p].at[r], "sd", r, p)
            for i in range(7):
                total = total + rd[p][r, i].astype(F32)
        t, n = parts[p]
        pt[p][r, x, zl] = gelu_slope(total, gl[r, :, t:t + n].astype(F32)).astype(BF16)
        own = pt[p].at[r, x, zl]
        if mode(gathers, r, p) == "d":
            for d, e in others:
                send(own, own, on_x(d, e), "pd", r, p)
        elif mode(gathers, r, p) == "t":
            for d in (2, 1, 3):
                send(own, own, on_x(d), "px", r, p, 0)
        else:
            send(own, own, zlp, "pz", r, p)

    def step_d(r, p):
        m = mode(gathers, r, p)
        if m == "t":
            arrived(rx[p].at[r], "px", r, p, 0)
            send(pt[p].at[r, :, zl], pt[p].at[r, :, zl], zlp, "pz", r, p)
        elif m != "d":
            arrived(pt[p].at[r, x, 1 - zl], "pz", r, p)
            for d in (1, 3) if m == "r" else (2, 1, 3):
                send(pt[p].at[r, x], pt[p].at[r, x], on_x(d), "px", r, p, d if m == "r" else 0)

    def step_v(r, p):
        if mode(gathers, r, p) == "r":
            for d in (1, 3):
                arrived(pt[p].at[r, xof(d)], "px", r, p, d)
                send(pt[p].at[r, xof(d), d // 2], pt[p].at[r, xof(d), d // 2], on_x(d), "pf", r, p)

    def step_e(r, p):
        m = mode(gathers, r, p)
        if m == "r":
            arrived(pt[p].at[r, xof(2)], "pf", r, p)
        elif m == "t":
            arrived(pt[p].at[r, :, 1 - zl], "pz", r, p)
        elif m == "s":
            arrived(rx2[p].at[r], "px", r, p, 0)
        else:
            arrived(rd[p].at[r], "pd", r, p)
        n = parts[p][1]
        for d in (2, 1, 3, 0):
            z = (zh + d) % 4
            rows = pl.ds(pl.multiple_of(z * 384, 384), 384)
            term = jnp.dot(wv[rows, :], pt[p][r].reshape(768, n), preferred_element_type=F32)
            dx[p][r, z] = term.astype(BF16).reshape(2, 192, n)
            send(dx[p].at[r, z, 1 - c], rc[p].at[r, z], core, "dc", r, p)

    def step_f(r, p):
        arrived(rc[p].at[r], "dc", r, p)
        if r % 2:
            arrived(rf[p].at[r // 2], "yf", r, p)
        for d in (2, 1, 3, 0):
            z = (zh + d) % 4
            total = dx[p][r, z, c].astype(F32) + rc[p][r, z].astype(F32)
            if r % 2:
                lo, hi = total[:96], total[96:]
                more = rf[p][r // 2, z].astype(F32)
                sy[p][r, z, halves[r]] = ((lo if r == 1 else hi) + more).astype(BF16)
                sy[p][r, z, halves[4 - r]] = (hi if r == 1 else lo).astype(BF16)
                send(sy[p].at[r, z], ry[p].at[r // 2, z], on_y(r), "dy", p, d)
            else:
                sy[p][r, z] = total.astype(BF16)
            if r == 2:
                for k in (1, 3):
                    send(sy[p].at[r, z, halves[k]], rf[p].at[k // 2, z], on_y(k), "yf", k, p)

    def step_m(i):
        total = None
        for r in range(4):
            for p, (_, n) in enumerate(parts):
                one = lax.dot_general(xt[p][r, 2 * i:2 * i + 2].reshape(768, n), pt[p][r].reshape(768, n), (((1,), (1,)), ((), ())),
                                      preferred_element_type=F32)
                total = one if total is None else total + one
        rows = pl.ds(i * 768, 768)
        dwv[rows, :] = total.astype(BF16)
        state["dw", i] = pltpu.make_async_copy(dwv.at[rows], dw_out.at[rows], lsem.at[1 if i else 3])
        state["dw", i].start()

    def step_s(d, p):
        z = (zh + d) % 4
        part = sy[p][0, z].astype(F32)
        arrived(ry[p].at[:, z], "dy", p, d)
        for k in range(2):
            part = part + ry[p][k, z].astype(F32)
        if d:
            sz[p][d] = part.astype(BF16)
            send(sz[p].at[d], rzz[p].at[d], on_z(d), "dz", p)
        else:
            state["own", p] = part

    def step_t(p):
        total = state["own", p]
        arrived(rzz[p].at[pl.ds(1, 3)], "dz", p)
        for d in (1, 2, 3):
            total = total + rzz[p][d].astype(F32)
        t, n = parts[p]
        dx_out[:, t:t + n] = total.astype(BF16)

    steps = dict(P=step_p, W=step_w, G=step_g, Z=step_z, Y=step_y, H=step_h, K=step_k, A=step_a, J=step_j, B=step_b, C=step_c,
                 D=step_d, V=step_v, E=step_e, F=step_f, M=step_m, S=step_s, T=step_t)
    for name in order:
        steps[name[0]](*map(int, name[1:]))

    for sent in sends[-N_SEND:]:
        sent()
    for i in range(2):
        state["dw", i].wait()
    assert not pending and len(keys) <= N_RECV, len(keys)


def copy_kernel(dx_in, dw_in, dx_out, dw_out, dx, dw, sems):
    spans = [(dw_in, dw, dw_out, pl.ds(i * 384, 384)) for i in range(4)] + [(dx_in, dx, dx_out, pl.ds(0, 192))]
    ins = [pltpu.make_async_copy(a.at[rows], b.at[rows], sems.at[0, i]) for i, (a, b, _, rows) in enumerate(spans)]
    outs = [pltpu.make_async_copy(b.at[rows], o.at[rows], sems.at[1, i]) for i, (_, b, o, rows) in enumerate(spans)]
    for cp in ins:
        cp.start()
    for cp, out in zip(ins, outs):
        cp.wait()
        out.start()
    for out in outs:
        out.wait()


SCRATCH = [(384, 384), (1536, 768), (768, 1536), (384, 384), (4, 96, 384), (1536, 768)]


def local(saved_input, weight, out_grad, order=ORDER, sums=SUM, gathers=GATHER, parts=PARTS, cid=0, name="fused_layer"):
    vmem = pl.BlockSpec(memory_space=pltpu.VMEM)
    shapes = SCRATCH + [s for _, n in parts for s in part_scratch(n).values()]
    dx, dw = pl.pallas_call(
        functools.partial(kernel, order, sums, gathers, parts),
        out_shape=[jax.ShapeDtypeStruct((192, 384), BF16), jax.ShapeDtypeStruct((1536, 768), BF16)],
        in_specs=[pl.BlockSpec(memory_space=pl.ANY)] * 3,
        out_specs=[vmem, pl.BlockSpec(memory_space=pl.ANY)],
        scratch_shapes=[pltpu.VMEM(s, BF16) for s in shapes] + [
            pltpu.SemaphoreType.DMA((N_SEND,)), pltpu.SemaphoreType.DMA((N_RECV,)), pltpu.SemaphoreType.DMA((8,)), pltpu.SemaphoreType.REGULAR((2,))],
        compiler_params=pltpu.CompilerParams(collective_id=cid, has_side_effects=True, vmem_limit_bytes=60 * 2**20),
        cost_estimate=pl.CostEstimate(flops=3 * 2 * 1536 * 1536 * 768, bytes_accessed=8 * 2**20, transcendentals=0),
        name=name,
    )(saved_input.T, weight, out_grad)
    hbm = pl.BlockSpec(memory_space=pl.ANY)
    dx, dw = pl.pallas_call(
        copy_kernel,
        out_shape=[jax.ShapeDtypeStruct((192, 384), BF16), jax.ShapeDtypeStruct((1536, 768), BF16)],
        in_specs=[hbm] * 2,
        out_specs=[hbm] * 2,
        scratch_shapes=[pltpu.VMEM((192, 384), BF16), pltpu.VMEM((1536, 768), BF16), pltpu.SemaphoreType.DMA((2, 5))],
        name="results",
    )(dx, dw)
    return dx.T, dw


def solution(mesh):
    placed = (P("gx", ("gy", "gz")), P("gy", ("gz", "gx")), P("gx", ("gz", "gy")))
    return jax.shard_map(
        local,
        mesh=mesh,
        in_specs=placed,
        out_specs=(P("gx", ("gy", "gz")), P("gy", ("gz", "gx"))),
        check_vma=False,
    )
```

```python
import functools

import jax
import jax.numpy as jnp
from jax import lax
from jax.experimental import pallas as pl
from jax.experimental.pallas import tpu as pltpu
from jax.sharding import PartitionSpec as P

MESH = pl.DeviceIdType.MESH
F32 = jnp.float32
BF16 = jnp.bfloat16
ROOT = 0.7978845608028654
CUBE = 0.044715
N_RECV = 89
N_SEND = 40

PARTS = ((0, 128), (128, 256))
ORDER = (
    "P", "W", "Y00", "Z30", "Y01", "Z10", "Y30", "Z11", "Z20", "Z31", "Y10", "K00", "A00", "Y20", "Y11", "Z21",
    "G", "H01", "K10", "A10", "H00", "H20", "K01", "H30", "A01", "H10", "K30", "H11", "Y31", "A30", "B00", "Y21",
    "K20", "A20", "B10", "K31", "A31", "B20", "K11", "B30", "A11", "H31", "H21", "C10", "K21", "A21", "C20",
    "D10", "C30", "B11", "C00", "D20", "V10", "B01", "B21", "V20", "E10", "D30", "C11", "B31", "E20", "V30",
    "C21", "D21", "F20", "D00", "C01", "E30", "D11", "C31", "V00", "F10", "F30", "V21", "E21", "D31", "E00",
    "F21", "V31", "V11", "F00", "S20", "S30", "D01", "E11", "E31", "F11", "F31", "S10", "V01", "E01", "F01",
    "S21", "S11", "S31", "M0", "M1", "S00", "T0", "S01", "T1",
)
SUM = "dxzxdzzz"
GATHER = "tssstdtd"


def gelu_slope(pre, grad):
    square = pre * pre
    tanh = jnp.tanh(ROOT * (pre + CUBE * (pre * square)))
    slope = 0.5 * (1.0 + tanh) + (0.5 * ROOT) * pre * (1.0 - tanh * tanh) * (1.0 + 3.0 * CUBE * square)
    return grad * slope


def part_scratch(n):
    return dict(
        xt=(4, 4, 2, 192, n),
        pp=(4, 4, 2, 96, n),
        rz=(4, 4, 96, n), s1=(4, 4, 96, n), rx=(4, 3, 96, n),
        rx2=(4, 3, 2, 96, n), s2=(4, 2, 96, n), rz2=(4, 96, n), rw=(4, 2, 96, n), sw=(4, 2, 2, 96, n),
        rd=(4, 7, 96, n),
        pt=(4, 4, 2, 96, n),
        dx=(4, 4, 2, 192, n),
        rc=(4, 4, 192, n), sy=(4, 4, 192, n), ry=(2, 4, 192, n), rf=(2, 4, 96, n),
        sz=(4, 192, n), rzz=(4, 192, n),
    )


def kernel(order, sums, gathers, parts, x_hbm, w_hbm, g_hbm, dx_out, dw_out, gv, wv, wt, gt, gl, dwv, *refs):
    ssem, rsem, lsem, near = refs[-4:]
    names = list(part_scratch(0))
    at = [dict(zip(names, refs[p * len(names):])) for p in range(len(parts))]
    xt, pp, rz, s1, rx, rx2, s2, rz2, rw, sw, rd, pt, dx, rc, sy, ry, rf, sz, rzz = ([a[n] for a in at] for n in names)

    y, gy, gz = lax.axis_index("gx"), lax.axis_index("gy"), lax.axis_index("gz")
    zl, x = gy // 4, gy % 4
    zh, c = gz // 2, gz % 2

    core = (y, gy, zh * 2 + (1 - c))
    zlp = (y, (1 - zl) * 4 + x, gz)

    def on_y(d):
        return ((y + d) % 4, gy, gz)

    def on_x(d, e=0):
        return (y, ((zl + e) % 2) * 4 + (x + d) % 4, gz)

    def on_z(d):
        return (y, gy, ((zh + d) % 4) * 2 + c)

    def zof(d):
        return (zh - d + 4) % 4

    def xof(d):
        return (x - d + 4) % 4

    g_dst = [(2 * zl + x // 2, z * 4 + 2 * (x % 2) + k, gz) for k in range(2) for z in range(2)]
    g_rows = [(2 * k + z) * 96 for k in range(2) for z in range(2)]
    own_g = jnp.logical_and(zl == y // 2, x == 2 * (y % 2) + x // 2)

    keys, sends, pending, state = {}, [], {}, {}
    others = ((2, 1), (2, 0), (1, 1), (1, 0), (3, 1), (3, 0), (0, 1))

    def mode(table, r, p):
        return table[r * len(parts) + p]

    def slot(*key):
        return keys.setdefault(key, len(keys))

    def send_slot():
        if len(sends) >= N_SEND:
            sends[-N_SEND]()
        return ssem.at[len(sends) % N_SEND]

    def send(src, dst, to, *key):
        cp = pltpu.make_async_remote_copy(src, dst, send_slot(), rsem.at[slot(*key)], device_id=to, device_id_type=MESH)
        cp.start()
        sends.append(cp.wait_send)
        pending.setdefault(key, []).append(dst)

    def arrived(ref, *key):
        assert ref.size == sum(dst.size for dst in pending.pop(key))
        k = slot(*key)
        pltpu.make_async_remote_copy(ref, ref, ssem.at[0], rsem.at[k], device_id=core, device_id_type=MESH).wait_recv()

    barrier = pltpu.get_barrier_semaphore()
    partners = [core, zlp] + [on_y(d) for d in (1, 2, 3)] + [on_x(d) for d in (1, 2, 3)] + [on_z(d) for d in (1, 3)]
    for to in partners:
        pl.semaphore_signal(barrier, inc=1, device_id=to, device_id_type=MESH)
    x_copies = [pltpu.make_async_copy(x_hbm.at[:, pl.ds(t, n)], xt[p].at[0, zh, c], lsem.at[5 + p])
                for p, (t, n) in enumerate(parts)]
    g_copy = pltpu.make_async_copy(g_hbm, gv, lsem.at[4])
    w_copy = pltpu.make_async_copy(w_hbm, wv, lsem.at[0])
    for cp in x_copies + [g_copy, w_copy]:
        cp.start()

    pl.semaphore_wait(barrier, len(partners))
    for d in (1, 2, 3):
        pl.semaphore_signal(near.at[0], inc=1, device_id=on_x(d), device_id_type=MESH)

    halves = {1: pl.ds(0, 96), 3: pl.ds(96, 96)}

    def step_p():
        for p in range(len(parts)):
            x_copies[p].wait()
            own = xt[p].at[0, zh, c]
            send(own, own, on_z(1), "z", 1, p)
            send(own, own, on_z(3), "z", 3, p)
            send(own, xt[p].at[3, zh, c], on_y(1), "y", 3, 0, p)
            send(own, xt[p].at[1, zh, c], on_y(3), "y", 1, 0, p)
            send(own, own, core, "k", 0, p)

    def step_w():
        g_copy.wait()
        gt[...] = gv[...].T
        w_copy.wait()

        @pl.loop(0, 2)
        def _(i):
            rows = pl.ds(pl.multiple_of(i * 768, 768), 768)
            wt[:, rows] = wv[rows, :].T
        pl.semaphore_wait(near.at[0], 3)
        for d in (1, 2, 3):
            pl.semaphore_signal(near.at[1], inc=1, device_id=on_y(d), device_id_type=MESH)

    def step_g():
        pl.semaphore_wait(near.at[1], 3)
        state["g"] = []
        for n in range(4):
            a, dgy, _ = g_dst[n]
            r = (y - a + 4) % 4
            here = jnp.logical_and(a == y, dgy == gy)
            src = gt.at[pl.ds(g_rows[n], 96)]
            cp = pltpu.make_async_remote_copy(src, gl.at[r], send_slot(), rsem.at[slot("g")], device_id=g_dst[n], device_id_type=MESH)
            lp = pltpu.make_async_copy(src, gl.at[0], lsem.at[2])

            @pl.when(jnp.logical_not(here))
            def _(cp=cp):
                cp.start()

            @pl.when(here)
            def _(lp=lp):
                lp.start()

            def sent(here=here, cp=cp):
                @pl.when(jnp.logical_not(here))
                def _():
                    cp.wait_send()
            sends.append(sent)
            state["g"].append((here, lp))

    def g_wait():
        if "g" not in state:
            return
        for here, lp in state.pop("g"):
            @pl.when(here)
            def _(lp=lp):
                lp.wait()
        k = slot("g")

        @pl.when(own_g)
        def _():
            part = gl.at[pl.ds(1, 3)]
            pltpu.make_async_remote_copy(part, part, ssem.at[0], rsem.at[k], device_id=core, device_id_type=MESH).wait_recv()

        @pl.when(jnp.logical_not(own_g))
        def _():
            pltpu.make_async_remote_copy(gl, gl, ssem.at[0], rsem.at[k], device_id=core, device_id_type=MESH).wait_recv()

    def step_z(d, p):
        shard = (zof(d), c)
        here = xt[p].at[(0,) + shard]
        if d == 2:
            arrived(here, "zf", p)
        else:
            arrived(here, "z", d, p)
            half = xt[p].at[(0,) + shard + (halves[d],)]
            send(half, half, on_z(d), "zf", p)
        send(here, xt[p].at[(3,) + shard], on_y(1), "y", 3, d, p)
        send(here, xt[p].at[(1,) + shard], on_y(3), "y", 1, d, p)
        send(here, here, core, "k", 0, p)

    def step_y(d, p):
        shard = (zof(d), c)
        for r, to in ((3, 1), (1, 3)):
            here = xt[p].at[(r,) + shard]
            arrived(here, "y", r, d, p)
            send(xt[p].at[(r,) + shard + (halves[to],)], xt[p].at[(2,) + shard + (halves[to],)], on_y(to), "f", d, p)
            send(here, here, core, "k", r, p)

    def step_h(d, p):
        shard = (zof(d), c)
        here = xt[p].at[(2,) + shard]
        arrived(here, "f", d, p)
        send(here, here, core, "k", 2, p)

    def step_k(r, p):
        arrived(xt[p].at[r, :, 1 - c], "k", r, p)

    def step_a(r, p):
        n = parts[p][1]
        term = jnp.dot(wt[...], xt[p][r].reshape(1536, n), preferred_element_type=F32)
        pp[p][r] = term.astype(BF16).reshape(4, 2, 96, n)
        m = mode(sums, r, p)
        if m == "x":
            for d in (2, 1, 3):
                send(pp[p].at[r, (x + d) % 4], rx2[p].at[r, d - 1], on_x(d), "sx", r, p)
        elif m == "w":
            for k, d in enumerate((1, 3)):
                send(pp[p].at[r, (x + 2) % 4, k], rw[p].at[r, k], on_x(d), "sw", r, p)
        elif m == "z":
            send(pp[p].at[r, :, 1 - zl], rz[p].at[r], zlp, "sz", r, p)
        else:
            for i, (d, e) in enumerate(others):
                send(pp[p].at[r, (x + d) % 4, (zl + e) % 2], rd[p].at[r, i], on_x(d, e), "sd", r, p)

    def step_j(r, p):
        if mode(sums, r, p) == "w":
            arrived(rw[p].at[r], "sw", r, p)
            for k, d in enumerate((1, 3)):
                sw[p][r, k, k] = (pp[p][r, (x + d) % 4, k].astype(F32) + rw[p][r, k].astype(F32)).astype(BF16)
                sw[p][r, k, 1 - k] = pp[p][r, (x + d) % 4, 1 - k]
                send(sw[p].at[r, k], rx2[p].at[r, k], on_x(d), "sx", r, p)

    def step_b(r, p):
        m = mode(sums, r, p)
        if m in "xw":
            total = pp[p][r, x].astype(F32)
            came = 3 if m == "x" else 2
            arrived(rx2[p].at[r, pl.ds(0, came)], "sx", r, p)
            for i in range(came):
                total = total + rx2[p][r, i].astype(F32)
            s2[p][r] = total.astype(BF16)
            send(s2[p].at[r, 1 - zl], rz2[p].at[r], zlp, "sz", r, p)
        elif m == "z":
            arrived(rz[p].at[r], "sz", r, p)
            s1[p][r] = (pp[p][r, :, zl].astype(F32) + rz[p][r].astype(F32)).astype(BF16)
            for d in (2, 1, 3):
                send(s1[p].at[r, (x + d) % 4], rx[p].at[r, d - 1], on_x(d), "sx", r, p)

    def step_c(r, p):
        g_wait()
        m = mode(sums, r, p)
        if m in "xw":
            arrived(rz2[p].at[r], "sz", r, p)
            total = s2[p][r, zl].astype(F32) + rz2[p][r].astype(F32)
        elif m == "z":
            total = s1[p][r, x].astype(F32)
            arrived(rx[p].at[r], "sx", r, p)
            for i in range(3):
                total = total + rx[p][r, i].astype(F32)
        else:
            total = pp[p][r, x, zl].astype(F32)
            arrived(rd[p].at[r], "sd", r, p)
            for i in range(7):
                total = total + rd[p][r, i].astype(F32)
        t, n = parts[p]
        pt[p][r, x, zl] = gelu_slope(total, gl[r, :, t:t + n].astype(F32)).astype(BF16)
        own = pt[p].at[r, x, zl]
        if mode(gathers, r, p) == "d":
            for d, e in others:
                send(own, own, on_x(d, e), "pd", r, p)
        elif mode(gathers, r, p) == "t":
            for d in (2, 1, 3):
                send(own, own, on_x(d), "px", r, p, 0)
        else:
            send(own, own, zlp, "pz", r, p)

    def step_d(r, p):
        m = mode(gathers, r, p)
        if m == "t":
            arrived(rx[p].at[r], "px", r, p, 0)
            send(pt[p].at[r, :, zl], pt[p].at[r, :, zl], zlp, "pz", r, p)
        elif m != "d":
            arrived(pt[p].at[r, x, 1 - zl], "pz", r, p)
            for d in (1, 3) if m == "r" else (2, 1, 3):
                send(pt[p].at[r, x], pt[p].at[r, x], on_x(d), "px", r, p, d if m == "r" else 0)

    def step_v(r, p):
        if mode(gathers, r, p) == "r":
            for d in (1, 3):
                arrived(pt[p].at[r, xof(d)], "px", r, p, d)
                send(pt[p].at[r, xof(d), d // 2], pt[p].at[r, xof(d), d // 2], on_x(d), "pf", r, p)

    def step_e(r, p):
        m = mode(gathers, r, p)
        if m == "r":
            arrived(pt[p].at[r, xof(2)], "pf", r, p)
        elif m == "t":
            arrived(pt[p].at[r, :, 1 - zl], "pz", r, p)
        elif m == "s":
            arrived(rx2[p].at[r], "px", r, p, 0)
        else:
            arrived(rd[p].at[r], "pd", r, p)
        n = parts[p][1]
        for d in (2, 1, 3, 0):
            z = (zh + d) % 4
            rows = pl.ds(pl.multiple_of(z * 384, 384), 384)
            term = jnp.dot(wv[rows, :], pt[p][r].reshape(768, n), preferred_element_type=F32)
            dx[p][r, z] = term.astype(BF16).reshape(2, 192, n)
            send(dx[p].at[r, z, 1 - c], rc[p].at[r, z], core, "dc", r, p)

    def step_f(r, p):
        arrived(rc[p].at[r], "dc", r, p)
        if r % 2:
            arrived(rf[p].at[r // 2], "yf", r, p)
        for d in (2, 1, 3, 0):
            z = (zh + d) % 4
            total = dx[p][r, z, c].astype(F32) + rc[p][r, z].astype(F32)
            if r % 2:
                lo, hi = total[:96], total[96:]
                more = rf[p][r // 2, z].astype(F32)
                sy[p][r, z, halves[r]] = ((lo if r == 1 else hi) + more).astype(BF16)
                sy[p][r, z, halves[4 - r]] = (hi if r == 1 else lo).astype(BF16)
                send(sy[p].at[r, z], ry[p].at[r // 2, z], on_y(r), "dy", p, d)
            else:
                sy[p][r, z] = total.astype(BF16)
            if r == 2:
                for k in (1, 3):
                    send(sy[p].at[r, z, halves[k]], rf[p].at[k // 2, z], on_y(k), "yf", k, p)

    def step_m(i):
        pieces = [(r, p, n) for r in range(4) for p, (_, n) in enumerate(parts)]
        lhs = jnp.concatenate([xt[p][r, 2 * i:2 * i + 2].reshape(768, n) for r, p, n in pieces], axis=1)
        rhs = jnp.concatenate([pt[p][r].reshape(768, n) for r, p, n in pieces], axis=1)
        total = lax.dot_general(lhs, rhs, (((1,), (1,)), ((), ())), preferred_element_type=F32)
        rows = pl.ds(i * 768, 768)
        dwv[rows, :] = total.astype(BF16)
        state["dw", i] = pltpu.make_async_copy(dwv.at[rows], dw_out.at[rows], lsem.at[1 if i else 3])
        state["dw", i].start()

    def step_s(d, p):
        z = (zh + d) % 4
        part = sy[p][0, z].astype(F32)
        arrived(ry[p].at[:, z], "dy", p, d)
        for k in range(2):
            part = part + ry[p][k, z].astype(F32)
        if d:
            sz[p][d] = part.astype(BF16)
            send(sz[p].at[d], rzz[p].at[d], on_z(d), "dz", p)
        else:
            state["own", p] = part

    def step_t(p):
        total = state["own", p]
        arrived(rzz[p].at[pl.ds(1, 3)], "dz", p)
        for d in (1, 2, 3):
            total = total + rzz[p][d].astype(F32)
        t, n = parts[p]
        dx_out[:, t:t + n] = total.astype(BF16)

    steps = dict(P=step_p, W=step_w, G=step_g, Z=step_z, Y=step_y, H=step_h, K=step_k, A=step_a, J=step_j, B=step_b, C=step_c,
                 D=step_d, V=step_v, E=step_e, F=step_f, M=step_m, S=step_s, T=step_t)
    for name in order:
        steps[name[0]](*map(int, name[1:]))

    for sent in sends[-N_SEND:]:
        sent()
    for i in range(2):
        state["dw", i].wait()
    assert not pending and len(keys) <= N_RECV, len(keys)


def copy_kernel(dx_in, dw_in, dx_out, dw_out, dx, dw, sems):
    spans = [(dw_in, dw, dw_out, pl.ds(i * 384, 384)) for i in range(4)] + [(dx_in, dx, dx_out, pl.ds(0, 192))]
    ins = [pltpu.make_async_copy(a.at[rows], b.at[rows], sems.at[0, i]) for i, (a, b, _, rows) in enumerate(spans)]
    outs = [pltpu.make_async_copy(b.at[rows], o.at[rows], sems.at[1, i]) for i, (_, b, o, rows) in enumerate(spans)]
    for cp in ins:
        cp.start()
    for cp, out in zip(ins, outs):
        cp.wait()
        out.start()
    for out in outs:
        out.wait()


SCRATCH = [(384, 384), (1536, 768), (768, 1536), (384, 384), (4, 96, 384), (1536, 768)]


def local(saved_input, weight, out_grad, order=ORDER, sums=SUM, gathers=GATHER, parts=PARTS, cid=0, name="fused_layer"):
    vmem = pl.BlockSpec(memory_space=pltpu.VMEM)
    shapes = SCRATCH + [s for _, n in parts for s in part_scratch(n).values()]
    dx, dw = pl.pallas_call(
        functools.partial(kernel, order, sums, gathers, parts),
        out_shape=[jax.ShapeDtypeStruct((192, 384), BF16), jax.ShapeDtypeStruct((1536, 768), BF16)],
        in_specs=[pl.BlockSpec(memory_space=pl.ANY)] * 3,
        out_specs=[vmem, pl.BlockSpec(memory_space=pl.ANY)],
        scratch_shapes=[pltpu.VMEM(s, BF16) for s in shapes] + [
            pltpu.SemaphoreType.DMA((N_SEND,)), pltpu.SemaphoreType.DMA((N_RECV,)), pltpu.SemaphoreType.DMA((8,)), pltpu.SemaphoreType.REGULAR((2,))],
        compiler_params=pltpu.CompilerParams(collective_id=cid, has_side_effects=True, vmem_limit_bytes=60 * 2**20),
        cost_estimate=pl.CostEstimate(flops=3 * 2 * 1536 * 1536 * 768, bytes_accessed=8 * 2**20, transcendentals=0),
        name=name,
    )(saved_input.T, weight, out_grad)
    hbm = pl.BlockSpec(memory_space=pl.ANY)
    dx, dw = pl.pallas_call(
        copy_kernel,
        out_shape=[jax.ShapeDtypeStruct((192, 384), BF16), jax.ShapeDtypeStruct((1536, 768), BF16)],
        in_specs=[hbm] * 2,
        out_specs=[hbm] * 2,
        scratch_shapes=[pltpu.VMEM((192, 384), BF16), pltpu.VMEM((1536, 768), BF16), pltpu.SemaphoreType.DMA((2, 5))],
        name="results",
    )(dx, dw)
    return dx.T, dw


def solution(mesh):
    placed = (P("gx", ("gy", "gz")), P("gy", ("gz", "gx")), P("gx", ("gz", "gy")))
    return jax.shard_map(
        local,
        mesh=mesh,
        in_specs=placed,
        out_specs=(P("gx", ("gy", "gz")), P("gy", ("gz", "gx"))),
        check_vma=False,
    )
```

```python
import functools

import jax
import jax.numpy as jnp
from jax import lax
from jax.experimental import pallas as pl
from jax.experimental.pallas import tpu as pltpu
from jax.sharding import PartitionSpec as P

MESH = pl.DeviceIdType.MESH
F32 = jnp.float32
BF16 = jnp.bfloat16
ROOT = 0.7978845608028654
CUBE = 0.044715
N_RECV = 89
N_SEND = 32

PARTS = ((0, 128), (128, 256))
ORDER = (
    "P", "W", "Y00", "Z30", "Y01", "Z10", "Y30", "Z11", "Z20", "Z31", "Y10", "K00", "A00", "Y20", "Y11", "Z21",
    "G", "H01", "K10", "A10", "H00", "H20", "K01", "H30", "A01", "H10", "K30", "H11", "Y31", "A30", "B00", "Y21",
    "K20", "A20", "B10", "K31", "A31", "B20", "K11", "B30", "A11", "H31", "H21", "C10", "K21", "A21", "C20",
    "D10", "C30", "B11", "C00", "D20", "V10", "B01", "B21", "V20", "E10", "D30", "C11", "B31", "E20", "V30",
    "C21", "D21", "F20", "D00", "C01", "E30", "D11", "C31", "V00", "F10", "F30", "V21", "E21", "D31", "E00",
    "F21", "V31", "V11", "F00", "S20", "S30", "D01", "E11", "E31", "F11", "F31", "S10", "V01", "E01", "F01",
    "S21", "S11", "S31", "M0", "M1", "S00", "T0", "S01", "T1",
)
SUM = "dxzxdzzz"
GATHER = "tssstdtd"


def gelu_slope(pre, grad):
    square = pre * pre
    tanh = jnp.tanh(ROOT * (pre + CUBE * (pre * square)))
    slope = 0.5 * (1.0 + tanh) + (0.5 * ROOT) * pre * (1.0 - tanh * tanh) * (1.0 + 3.0 * CUBE * square)
    return grad * slope


def part_scratch(n):
    return dict(
        xt=(4, 4, 2, 192, n),
        pp=(4, 4, 2, 96, n),
        rz=(4, 4, 96, n), s1=(4, 4, 96, n), rx=(4, 3, 96, n),
        rx2=(4, 3, 2, 96, n), s2=(4, 2, 96, n), rz2=(4, 96, n), rw=(4, 2, 96, n), sw=(4, 2, 2, 96, n),
        rd=(4, 7, 96, n),
        pt=(4, 4, 2, 96, n),
        dx=(4, 4, 2, 192, n),
        rc=(4, 4, 192, n), sy=(4, 4, 192, n), ry=(2, 4, 192, n), rf=(2, 4, 96, n),
        sz=(4, 192, n), rzz=(4, 192, n),
    )


def kernel(order, sums, gathers, parts, x_hbm, w_hbm, g_hbm, dx_out, dw_out, gv, wv, wt, gt, gl, dwv, *refs):
    ssem, rsem, lsem, near = refs[-4:]
    names = list(part_scratch(0))
    at = [dict(zip(names, refs[p * len(names):])) for p in range(len(parts))]
    xt, pp, rz, s1, rx, rx2, s2, rz2, rw, sw, rd, pt, dx, rc, sy, ry, rf, sz, rzz = ([a[n] for a in at] for n in names)

    y, gy, gz = lax.axis_index("gx"), lax.axis_index("gy"), lax.axis_index("gz")
    zl, x = gy // 4, gy % 4
    zh, c = gz // 2, gz % 2

    core = (y, gy, zh * 2 + (1 - c))
    zlp = (y, (1 - zl) * 4 + x, gz)

    def on_y(d):
        return ((y + d) % 4, gy, gz)

    def on_x(d, e=0):
        return (y, ((zl + e) % 2) * 4 + (x + d) % 4, gz)

    def on_z(d):
        return (y, gy, ((zh + d) % 4) * 2 + c)

    def zof(d):
        return (zh - d + 4) % 4

    def xof(d):
        return (x - d + 4) % 4

    g_dst = [(2 * zl + x // 2, z * 4 + 2 * (x % 2) + k, gz) for k in range(2) for z in range(2)]
    g_rows = [(2 * k + z) * 96 for k in range(2) for z in range(2)]
    own_g = jnp.logical_and(zl == y // 2, x == 2 * (y % 2) + x // 2)

    keys, sends, pending, state = {}, [], {}, {}
    others = ((2, 1), (2, 0), (1, 1), (1, 0), (3, 1), (3, 0), (0, 1))

    def mode(table, r, p):
        return table[r * len(parts) + p]

    def slot(*key):
        return keys.setdefault(key, len(keys))

    def send_slot():
        if len(sends) >= N_SEND:
            sends[-N_SEND]()
        return ssem.at[len(sends) % N_SEND]

    def send(src, dst, to, *key):
        cp = pltpu.make_async_remote_copy(src, dst, send_slot(), rsem.at[slot(*key)], device_id=to, device_id_type=MESH)
        cp.start()
        sends.append(cp.wait_send)
        pending.setdefault(key, []).append(dst)

    def arrived(ref, *key):
        assert ref.size == sum(dst.size for dst in pending.pop(key))
        k = slot(*key)
        pltpu.make_async_remote_copy(ref, ref, ssem.at[0], rsem.at[k], device_id=core, device_id_type=MESH).wait_recv()

    barrier = pltpu.get_barrier_semaphore()
    partners = [core, zlp] + [on_y(d) for d in (1, 2, 3)] + [on_x(d) for d in (1, 2, 3)] + [on_z(d) for d in (1, 3)]
    for to in partners:
        pl.semaphore_signal(barrier, inc=1, device_id=to, device_id_type=MESH)
    x_copies = [pltpu.make_async_copy(x_hbm.at[:, pl.ds(t, n)], xt[p].at[0, zh, c], lsem.at[5 + p])
                for p, (t, n) in enumerate(parts)]
    g_copy = pltpu.make_async_copy(g_hbm, gv, lsem.at[4])
    w_copy = pltpu.make_async_copy(w_hbm, wv, lsem.at[0])
    for cp in x_copies + [g_copy, w_copy]:
        cp.start()

    pl.semaphore_wait(barrier, len(partners))
    for d in (1, 2, 3):
        pl.semaphore_signal(near.at[0], inc=1, device_id=on_x(d), device_id_type=MESH)

    halves = {1: pl.ds(0, 96), 3: pl.ds(96, 96)}

    def step_p():
        for p in range(len(parts)):
            x_copies[p].wait()
            own = xt[p].at[0, zh, c]
            send(own, own, on_z(1), "z", 1, p)
            send(own, own, on_z(3), "z", 3, p)
            send(own, xt[p].at[3, zh, c], on_y(1), "y", 3, 0, p)
            send(own, xt[p].at[1, zh, c], on_y(3), "y", 1, 0, p)
            send(own, own, core, "k", 0, p)

    def step_w():
        g_copy.wait()
        gt[...] = gv[...].T
        w_copy.wait()

        @pl.loop(0, 2)
        def _(i):
            rows = pl.ds(pl.multiple_of(i * 768, 768), 768)
            wt[:, rows] = wv[rows, :].T
        pl.semaphore_wait(near.at[0], 3)
        for d in (1, 2, 3):
            pl.semaphore_signal(near.at[1], inc=1, device_id=on_y(d), device_id_type=MESH)

    def step_g():
        pl.semaphore_wait(near.at[1], 3)
        state["g"] = []
        for n in range(4):
            a, dgy, _ = g_dst[n]
            r = (y - a + 4) % 4
            here = jnp.logical_and(a == y, dgy == gy)
            src = gt.at[pl.ds(g_rows[n], 96)]
            cp = pltpu.make_async_remote_copy(src, gl.at[r], send_slot(), rsem.at[slot("g")], device_id=g_dst[n], device_id_type=MESH)
            lp = pltpu.make_async_copy(src, gl.at[0], lsem.at[2])

            @pl.when(jnp.logical_not(here))
            def _(cp=cp):
                cp.start()

            @pl.when(here)
            def _(lp=lp):
                lp.start()

            def sent(here=here, cp=cp):
                @pl.when(jnp.logical_not(here))
                def _():
                    cp.wait_send()
            sends.append(sent)
            state["g"].append((here, lp))

    def g_wait():
        if "g" not in state:
            return
        for here, lp in state.pop("g"):
            @pl.when(here)
            def _(lp=lp):
                lp.wait()
        k = slot("g")

        @pl.when(own_g)
        def _():
            part = gl.at[pl.ds(1, 3)]
            pltpu.make_async_remote_copy(part, part, ssem.at[0], rsem.at[k], device_id=core, device_id_type=MESH).wait_recv()

        @pl.when(jnp.logical_not(own_g))
        def _():
            pltpu.make_async_remote_copy(gl, gl, ssem.at[0], rsem.at[k], device_id=core, device_id_type=MESH).wait_recv()

    def step_z(d, p):
        shard = (zof(d), c)
        here = xt[p].at[(0,) + shard]
        if d == 2:
            arrived(here, "zf", p)
        else:
            arrived(here, "z", d, p)
            half = xt[p].at[(0,) + shard + (halves[d],)]
            send(half, half, on_z(d), "zf", p)
        send(here, xt[p].at[(3,) + shard], on_y(1), "y", 3, d, p)
        send(here, xt[p].at[(1,) + shard], on_y(3), "y", 1, d, p)
        send(here, here, core, "k", 0, p)

    def step_y(d, p):
        shard = (zof(d), c)
        for r, to in ((3, 1), (1, 3)):
            here = xt[p].at[(r,) + shard]
            arrived(here, "y", r, d, p)
            send(xt[p].at[(r,) + shard + (halves[to],)], xt[p].at[(2,) + shard + (halves[to],)], on_y(to), "f", d, p)
            send(here, here, core, "k", r, p)

    def step_h(d, p):
        shard = (zof(d), c)
        here = xt[p].at[(2,) + shard]
        arrived(here, "f", d, p)
        send(here, here, core, "k", 2, p)

    def step_k(r, p):
        arrived(xt[p].at[r, :, 1 - c], "k", r, p)

    def step_a(r, p):
        n = parts[p][1]
        term = jnp.dot(wt[...], xt[p][r].reshape(1536, n), preferred_element_type=F32)
        pp[p][r] = term.astype(BF16).reshape(4, 2, 96, n)
        m = mode(sums, r, p)
        if m == "x":
            for d in (2, 1, 3):
                send(pp[p].at[r, (x + d) % 4], rx2[p].at[r, d - 1], on_x(d), "sx", r, p)
        elif m == "w":
            for k, d in enumerate((1, 3)):
                send(pp[p].at[r, (x + 2) % 4, k], rw[p].at[r, k], on_x(d), "sw", r, p)
        elif m == "z":
            send(pp[p].at[r, :, 1 - zl], rz[p].at[r], zlp, "sz", r, p)
        else:
            for i, (d, e) in enumerate(others):
                send(pp[p].at[r, (x + d) % 4, (zl + e) % 2], rd[p].at[r, i], on_x(d, e), "sd", r, p)

    def step_j(r, p):
        if mode(sums, r, p) == "w":
            arrived(rw[p].at[r], "sw", r, p)
            for k, d in enumerate((1, 3)):
                sw[p][r, k, k] = (pp[p][r, (x + d) % 4, k].astype(F32) + rw[p][r, k].astype(F32)).astype(BF16)
                sw[p][r, k, 1 - k] = pp[p][r, (x + d) % 4, 1 - k]
                send(sw[p].at[r, k], rx2[p].at[r, k], on_x(d), "sx", r, p)

    def step_b(r, p):
        m = mode(sums, r, p)
        if m in "xw":
            total = pp[p][r, x].astype(F32)
            came = 3 if m == "x" else 2
            arrived(rx2[p].at[r, pl.ds(0, came)], "sx", r, p)
            for i in range(came):
                total = total + rx2[p][r, i].astype(F32)
            s2[p][r] = total.astype(BF16)
            send(s2[p].at[r, 1 - zl], rz2[p].at[r], zlp, "sz", r, p)
        elif m == "z":
            arrived(rz[p].at[r], "sz", r, p)
            s1[p][r] = (pp[p][r, :, zl].astype(F32) + rz[p][r].astype(F32)).astype(BF16)
            for d in (2, 1, 3):
                send(s1[p].at[r, (x + d) % 4], rx[p].at[r, d - 1], on_x(d), "sx", r, p)

    def step_c(r, p):
        g_wait()
        m = mode(sums, r, p)
        if m in "xw":
            arrived(rz2[p].at[r], "sz", r, p)
            total = s2[p][r, zl].astype(F32) + rz2[p][r].astype(F32)
        elif m == "z":
            total = s1[p][r, x].astype(F32)
            arrived(rx[p].at[r], "sx", r, p)
            for i in range(3):
                total = total + rx[p][r, i].astype(F32)
        else:
            total = pp[p][r, x, zl].astype(F32)
            arrived(rd[p].at[r], "sd", r, p)
            for i in range(7):
                total = total + rd[p][r, i].astype(F32)
        t, n = parts[p]
        pt[p][r, x, zl] = gelu_slope(total, gl[r, :, t:t + n].astype(F32)).astype(BF16)
        own = pt[p].at[r, x, zl]
        if mode(gathers, r, p) == "d":
            for d, e in others:
                send(own, own, on_x(d, e), "pd", r, p)
        elif mode(gathers, r, p) == "t":
            for d in (2, 1, 3):
                send(own, own, on_x(d), "px", r, p, 0)
        else:
            send(own, own, zlp, "pz", r, p)

    def step_d(r, p):
        m = mode(gathers, r, p)
        if m == "t":
            arrived(rx[p].at[r], "px", r, p, 0)
            send(pt[p].at[r, :, zl], pt[p].at[r, :, zl], zlp, "pz", r, p)
        elif m != "d":
            arrived(pt[p].at[r, x, 1 - zl], "pz", r, p)
            for d in (1, 3) if m == "r" else (2, 1, 3):
                send(pt[p].at[r, x], pt[p].at[r, x], on_x(d), "px", r, p, d if m == "r" else 0)

    def step_v(r, p):
        if mode(gathers, r, p) == "r":
            for d in (1, 3):
                arrived(pt[p].at[r, xof(d)], "px", r, p, d)
                send(pt[p].at[r, xof(d), d // 2], pt[p].at[r, xof(d), d // 2], on_x(d), "pf", r, p)

    def step_e(r, p):
        m = mode(gathers, r, p)
        if m == "r":
            arrived(pt[p].at[r, xof(2)], "pf", r, p)
        elif m == "t":
            arrived(pt[p].at[r, :, 1 - zl], "pz", r, p)
        elif m == "s":
            arrived(rx2[p].at[r], "px", r, p, 0)
        else:
            arrived(rd[p].at[r], "pd", r, p)
        n = parts[p][1]
        for d in (2, 1, 3, 0):
            z = (zh + d) % 4
            rows = pl.ds(pl.multiple_of(z * 384, 384), 384)
            term = jnp.dot(wv[rows, :], pt[p][r].reshape(768, n), preferred_element_type=F32)
            dx[p][r, z] = term.astype(BF16).reshape(2, 192, n)
            send(dx[p].at[r, z, 1 - c], rc[p].at[r, z], core, "dc", r, p)

    def step_f(r, p):
        arrived(rc[p].at[r], "dc", r, p)
        if r % 2:
            arrived(rf[p].at[r // 2], "yf", r, p)
        for d in (2, 1, 3, 0):
            z = (zh + d) % 4
            total = dx[p][r, z, c].astype(F32) + rc[p][r, z].astype(F32)
            if r % 2:
                lo, hi = total[:96], total[96:]
                more = rf[p][r // 2, z].astype(F32)
                sy[p][r, z, halves[r]] = ((lo if r == 1 else hi) + more).astype(BF16)
                sy[p][r, z, halves[4 - r]] = (hi if r == 1 else lo).astype(BF16)
                send(sy[p].at[r, z], ry[p].at[r // 2, z], on_y(r), "dy", p, d)
            else:
                sy[p][r, z] = total.astype(BF16)
            if r == 2:
                for k in (1, 3):
                    send(sy[p].at[r, z, halves[k]], rf[p].at[k // 2, z], on_y(k), "yf", k, p)

    def step_m(i):
        pieces = [(r, p, n) for r in range(4) for p, (_, n) in enumerate(parts)]
        lhs = jnp.concatenate([xt[p][r, 2 * i:2 * i + 2].reshape(768, n) for r, p, n in pieces], axis=1)
        rhs = jnp.concatenate([pt[p][r].reshape(768, n) for r, p, n in pieces], axis=1)
        total = lax.dot_general(lhs, rhs, (((1,), (1,)), ((), ())), preferred_element_type=F32)
        rows = pl.ds(i * 768, 768)
        dwv[rows, :] = total.astype(BF16)
        state["dw", i] = pltpu.make_async_copy(dwv.at[rows], dw_out.at[rows], lsem.at[1 if i else 3])
        state["dw", i].start()

    def step_s(d, p):
        z = (zh + d) % 4
        part = sy[p][0, z].astype(F32)
        arrived(ry[p].at[:, z], "dy", p, d)
        for k in range(2):
            part = part + ry[p][k, z].astype(F32)
        if d:
            sz[p][d] = part.astype(BF16)
            send(sz[p].at[d], rzz[p].at[d], on_z(d), "dz", p)
        else:
            state["own", p] = part

    def step_t(p):
        total = state["own", p]
        arrived(rzz[p].at[pl.ds(1, 3)], "dz", p)
        for d in (1, 2, 3):
            total = total + rzz[p][d].astype(F32)
        t, n = parts[p]
        sz[p][0] = total.astype(BF16)
        state["dx", p] = pltpu.make_async_copy(sz[p].at[0], dx_out.at[:, pl.ds(t, n)], lsem.at[5 + p])
        state["dx", p].start()

    steps = dict(P=step_p, W=step_w, G=step_g, Z=step_z, Y=step_y, H=step_h, K=step_k, A=step_a, J=step_j, B=step_b, C=step_c,
                 D=step_d, V=step_v, E=step_e, F=step_f, M=step_m, S=step_s, T=step_t)
    for name in order:
        steps[name[0]](*map(int, name[1:]))

    for sent in sends[-N_SEND:]:
        sent()
    for i in range(2):
        state["dw", i].wait()
    for p in range(len(parts)):
        state["dx", p].wait()
    assert not pending and len(keys) <= N_RECV, len(keys)


def copy_kernel(dx_in, dw_in, dx_out, dw_out, dx, dw, sems):
    spans = [(dw_in, dw, dw_out, pl.ds(i * 384, 384)) for i in range(4)] + [(dx_in, dx, dx_out, pl.ds(0, 192))]
    ins = [pltpu.make_async_copy(a.at[rows], b.at[rows], sems.at[0, i]) for i, (a, b, _, rows) in enumerate(spans)]
    outs = [pltpu.make_async_copy(b.at[rows], o.at[rows], sems.at[1, i]) for i, (_, b, o, rows) in enumerate(spans)]
    for cp in ins:
        cp.start()
    for cp, out in zip(ins, outs):
        cp.wait()
        out.start()
    for out in outs:
        out.wait()


SCRATCH = [(384, 384), (1536, 768), (768, 1536), (384, 384), (4, 96, 384), (1536, 768)]


def local(saved_input, weight, out_grad, order=ORDER, sums=SUM, gathers=GATHER, parts=PARTS, cid=0, name="fused_layer"):
    shapes = SCRATCH + [s for _, n in parts for s in part_scratch(n).values()]
    dx, dw = pl.pallas_call(
        functools.partial(kernel, order, sums, gathers, parts),
        out_shape=[jax.ShapeDtypeStruct((192, 384), BF16), jax.ShapeDtypeStruct((1536, 768), BF16)],
        in_specs=[pl.BlockSpec(memory_space=pl.ANY)] * 3,
        out_specs=[pl.BlockSpec(memory_space=pl.ANY)] * 2,
        scratch_shapes=[pltpu.VMEM(s, BF16) for s in shapes] + [
            pltpu.SemaphoreType.DMA((N_SEND,)), pltpu.SemaphoreType.DMA((N_RECV,)), pltpu.SemaphoreType.DMA((8,)), pltpu.SemaphoreType.REGULAR((2,))],
        compiler_params=pltpu.CompilerParams(collective_id=cid, has_side_effects=True, vmem_limit_bytes=60 * 2**20),
        cost_estimate=pl.CostEstimate(flops=3 * 2 * 1536 * 1536 * 768, bytes_accessed=8 * 2**20, transcendentals=0),
        name=name,
    )(saved_input.T, weight, out_grad)
    hbm = pl.BlockSpec(memory_space=pl.ANY)
    dx, dw = pl.pallas_call(
        copy_kernel,
        out_shape=[jax.ShapeDtypeStruct((192, 384), BF16), jax.ShapeDtypeStruct((1536, 768), BF16)],
        in_specs=[hbm] * 2,
        out_specs=[hbm] * 2,
        scratch_shapes=[pltpu.VMEM((192, 384), BF16), pltpu.VMEM((1536, 768), BF16), pltpu.SemaphoreType.DMA((2, 5))],
        name="results",
    )(dx, dw)
    return dx.T, dw


def solution(mesh):
    placed = (P("gx", ("gy", "gz")), P("gy", ("gz", "gx")), P("gx", ("gz", "gy")))
    return jax.shard_map(
        local,
        mesh=mesh,
        in_specs=placed,
        out_specs=(P("gx", ("gy", "gz")), P("gy", ("gz", "gx"))),
        check_vma=False,
    )
```
